32 devices in a mesh: section: 2 (over y), tensor: 2 (over x), dp: 8 (over z, core).
Axes of the slice: x: 2, y: 2, z: 4, core: 2. Of those that a mesh axis runs over, the one named last changes fastest.
Arguments:
- query_rows: bfloat16 [8192, 8192], P(('section', 'dp'), 'tensor'), may hold values from -108 to 108
- key_rows: bfloat16 [8192, 1024], P(('section', 'dp'), 'tensor'), may hold values from -4.5 to 4.5
- rows_of_values: bfloat16 [8192, 1024], P(('section', 'dp'), 'tensor'), may hold values from -6 to 6
- cached_key_rows: bfloat16 [1024, 16, 1024], P('dp', None, 'tensor'), may hold values from -6 to 6
- cached_value_rows: bfloat16 [1024, 16, 1024], P('dp', None, 'tensor'), may hold values from -6 to 6
- cache_lengths: int32 [1024], P('dp'), may hold values from 1 to 16, 8192 in all
- prompt_lengths: int32 [4], replicated, may hold values from 1 to 2048, 4096 in all
- owners: int32 [4], replicated, may hold values from 0 to 7, as said below
- out_weight: bfloat16 [8192, 5120], P('tensor'), may hold values from -0.25 to 0.25
Outputs:
- layer_rows: bfloat16 [8192, 5120], P(('section', 'dp'), 'tensor')
The draws below stay inside these ranges and needn't reach their ends.
Inputs may be any that keep to these rules, and one draw needn't show every extreme that they name: `cache_lengths`: the cached positions of a request number 1 to 16; the largest is 16. `prompt_lengths`: the prompt lengths sum to 4096; the longest is 2048. The owners of the new requests are distinct.
All inputs are finite; a program needn't handle non-finite values. No bound on the sum of `cache_lengths` on one device may be relied on, other than what follows from the above.
Results may differ from the reference program's by a relative error of at most 0.013.
Values may be sent and summed in bfloat16 or wider, within the bound.
A program may use at most 256 MiB of HBM per device.

```python
import math
import jax
import jax.numpy as jnp
import numpy as np
from jax import lax

D = 5120
QUERY_HEADS = 64
KEY_VALUE_HEADS = 8
HEAD_SIZE = 128
TOK_DEV = 512
STEPS = 4
CACHE_POSITIONS = 16
MAXLEN = 2048
REQ_DEV = 128
DECODE_REQUESTS = 1024
PROMPT_TOKENS = 4096
NEW_REQS = 4
N_TENSOR = 2
N_DP = 8


def shared_rows(key):
    return jax.random.truncated_normal(key, -4.5, 4.5, (2 * PROMPT_TOKENS, KEY_VALUE_HEADS * HEAD_SIZE), jnp.float32)


def draw_key_rows(key, part):
    starting_rows = shared_rows(key)
    return starting_rows.astype(jnp.bfloat16)


def draw_query_rows(key, part):
    starting_rows = shared_rows(key)
    own_key = jax.random.fold_in(key, 7)
    total_rows = 2 * PROMPT_TOKENS
    noise = jax.random.truncated_normal(own_key, -4.5, 4.5, (total_rows, QUERY_HEADS * HEAD_SIZE), jnp.float32)
    repeated_heads = jnp.repeat(starting_rows.reshape(total_rows, KEY_VALUE_HEADS, 1, HEAD_SIZE), QUERY_HEADS // KEY_VALUE_HEADS, axis=2).reshape(total_rows, QUERY_HEADS * HEAD_SIZE)
    queries = 0.3 * repeated_heads + 0.95 * noise
    return queries.astype(jnp.bfloat16)


def draw_owners(key, part):
    key = jax.random.fold_in(key, 31)
    middle = jax.random.permutation(jax.random.fold_in(key, 1), N_DP - 2)[:NEW_REQS - 2] + 1
    picked = jnp.concatenate([jnp.array([0, N_DP - 1], jnp.int32), middle.astype(jnp.int32)])
    arrangement = jax.random.permutation(jax.random.fold_in(key, 2), NEW_REQS)
    return picked[arrangement].astype(jnp.int32)


def level_of(key, shape, shards, least, top_value):
    gain = 1.0
    for dim, shards_of in shards:
        draws = jax.random.uniform(jax.random.fold_in(jax.random.fold_in(key, 6), dim), (shards_of,), jnp.float32, least / len(shards), top_value / len(shards))
        gain = gain * jnp.repeat(jnp.exp(draws), shape[dim] // shards_of).reshape((-1,) + (1,) * (len(shape) - 1 - dim))
    return gain


def split_up(number_of, total, reach, slope):
    weights = [(1 << 20) // math.isqrt(rank ** slope) + 1 for rank in range(2, number_of + 1)]
    rest, given = total - reach - (number_of - 1), [1] * (number_of - 1)
    while rest > 0:
        candidates = [i for i in range(number_of - 1) if given[i] < reach]
        whole, left = sum([weights[i] for i in candidates]), rest
        for i in candidates:
            extra = min(reach - given[i], max(1, left * weights[i] // whole), rest)
            given[i] = given[i] + extra
            rest = rest - extra
    return np.array([reach] + given)


def uneven(key, amount, total, reach, skew):
    if amount == 2:
        one = jax.random.randint(key, (), max(1, total - reach), min(reach, total - 1) + 1)
        return jnp.stack([one, total - one])
    sizes = jnp.asarray(split_up(amount, total, reach, skew), jnp.int32)
    couples = (amount - 1) // 2
    source_of, sink = sizes[1:1 + 2 * couples:2], sizes[2:2 + 2 * couples:2]
    slack = jnp.minimum(source_of - 1, reach - sink)
    shifted = jax.random.randint(jax.random.fold_in(key, 1), (couples,), 0, 1 << 20) % (slack + 1)
    sizes = sizes.at[1:1 + 2 * couples:2].set(source_of - shifted).at[2:2 + 2 * couples:2].set(sink + shifted)
    return sizes[jax.random.permutation(jax.random.fold_in(key, 2), amount)]


def bell_draw(key, extent, width, bound, split=(), held_as=jnp.bfloat16):
    values = jax.random.normal(key, extent, jnp.float32) * width
    if len(split) > 0:
        values = level_of(key, extent, split, -0.22, 0.18) * values
    return jnp.clip(values, min=-bound, max=bound).astype(held_as)


def setup_inputs(seed: int = 0) -> dict:
    splits = jax.random.split(jax.random.key(seed), 10)
    query_rows = draw_query_rows(jax.random.fold_in(splits[9], 71), 0)
    key_rows = draw_key_rows(jax.random.fold_in(splits[9], 71), 0)
    rows_of_values = bell_draw(splits[2], (2 * PROMPT_TOKENS, KEY_VALUE_HEADS * HEAD_SIZE), 1.0, 6.0, ((0, 16), (1, 2)))
    cached_key_rows = bell_draw(splits[3], (DECODE_REQUESTS, CACHE_POSITIONS, KEY_VALUE_HEADS * HEAD_SIZE), 1.0, 6.0, ((0, 8), (2, 2)))
    cached_value_rows = bell_draw(splits[4], (DECODE_REQUESTS, CACHE_POSITIONS, KEY_VALUE_HEADS * HEAD_SIZE), 1.0, 6.0, ((0, 8), (2, 2)))
    cache_lengths = uneven(splits[5], DECODE_REQUESTS, DECODE_REQUESTS * CACHE_POSITIONS // 2, CACHE_POSITIONS, 1).astype(jnp.int32)
    prompt_lengths = uneven(splits[6], NEW_REQS, PROMPT_TOKENS, MAXLEN, 2).astype(jnp.int32)
    owners = draw_owners(jax.random.fold_in(splits[9], 71), 0)
    out_weight = bell_draw(splits[8], (QUERY_HEADS * HEAD_SIZE, D), (QUERY_HEADS * HEAD_SIZE // 16) ** -0.5, 0.25, ((0, 2),))
    return {"query_rows": query_rows, "key_rows": key_rows, "rows_of_values": rows_of_values, "cached_key_rows": cached_key_rows, "cached_value_rows": cached_value_rows, "cache_lengths": cache_lengths, "prompt_lengths": prompt_lengths, "owners": owners, "out_weight": out_weight}


masked_score = -1e30


def attend_rows(queries, key_block, value_block, allowed):
    row_count = queries.shape[0]
    key_count = key_block.shape[0]
    heads_kv = key_block.shape[1] // HEAD_SIZE
    group_size = queries.shape[1] // key_block.shape[1]
    query_heads = queries.astype(jnp.float32).reshape(row_count, heads_kv, group_size, HEAD_SIZE)
    key_heads = key_block.astype(jnp.float32).reshape(key_count, heads_kv, HEAD_SIZE)
    value_heads = value_block.astype(jnp.float32).reshape(key_count, heads_kv, HEAD_SIZE)
    scores = jnp.einsum("rkgd,wkd->kgrw", query_heads, key_heads) * (HEAD_SIZE ** -0.5)
    scores = jnp.where(allowed[None, None], scores, masked_score)
    row_max = jnp.max(scores, axis=-1, keepdims=True)
    exponent = jnp.exp(scores - row_max)
    weights = (exponent / jnp.sum(exponent, axis=-1, keepdims=True)).astype(jnp.bfloat16)
    mixed = jnp.einsum("kgrw,wkd->rkgd", weights.astype(jnp.float32), value_heads)
    return mixed.reshape(row_count, -1).astype(jnp.bfloat16)


def attend_slots(queries, key_block, value_block, lower, upper, context):
    step_count = queries.shape[1]
    key_count = key_block.shape[1]
    position = jnp.arange(key_count, dtype=jnp.int32)
    step_index = jnp.arange(step_count, dtype=jnp.int32)
    inside = (position[None, None, :] >= lower[:, None, None]) & (position[None, None, :] < upper[:, None, None]) & (position[None, None, :] < context)
    own_steps = (position[None, None, :] >= context) & (position[None, None, :] - context <= step_index[None, :, None])
    return jax.vmap(attend_rows)(queries, key_block, value_block, inside | own_steps)


def reference(query_rows, key_rows, rows_of_values, cached_key_rows, cached_value_rows, cache_lengths, prompt_lengths, owners, out_weight):
    prompt_total = PROMPT_TOKENS
    key_window = MAXLEN + TOK_DEV
    starts = (jnp.cumsum(prompt_lengths) - prompt_lengths).astype(jnp.int32)
    prompt_keys = key_rows[:prompt_total]
    prompt_values = rows_of_values[:prompt_total]

    def prefill_block(block_index):
        first_row = (block_index * TOK_DEV).astype(jnp.int32)
        window_start = jnp.clip(first_row - MAXLEN, 0, prompt_total - key_window).astype(jnp.int32)
        queries = lax.dynamic_slice_in_dim(query_rows, first_row, TOK_DEV, 0)
        key_block = lax.dynamic_slice_in_dim(prompt_keys, window_start, key_window, 0)
        value_block = lax.dynamic_slice_in_dim(prompt_values, window_start, key_window, 0)
        query_pos = first_row + jnp.arange(TOK_DEV, dtype=jnp.int32)
        query_start = jnp.max(jnp.where(starts[None, :] <= query_pos[:, None], starts[None, :], 0), axis=1)
        key_pos = window_start + jnp.arange(key_window, dtype=jnp.int32)
        allowed = (key_pos[None, :] >= query_start[:, None]) & (key_pos[None, :] <= query_pos[:, None])
        return attend_rows(queries, key_block, value_block, allowed)

    prefill = lax.map(prefill_block, jnp.arange(N_DP, dtype=jnp.int32)).reshape(prompt_total, -1)

    decode_queries = query_rows[prompt_total:].reshape(N_DP, REQ_DEV, STEPS, -1)
    decode_keys = key_rows[prompt_total:].reshape(N_DP, REQ_DEV, STEPS, -1)
    decode_values = rows_of_values[prompt_total:].reshape(N_DP, REQ_DEV, STEPS, -1)
    owner_cache_keys = cached_key_rows.reshape(N_DP, REQ_DEV, CACHE_POSITIONS, -1)
    owner_cache_values = cached_value_rows.reshape(N_DP, REQ_DEV, CACHE_POSITIONS, -1)
    owner_lengths = cache_lengths.reshape(N_DP, REQ_DEV)

    def decode_owner(bundle):
        owner_id, step_queries, step_keys, step_values, own_keys, own_values, own_lengths = bundle
        is_owner = (owners == owner_id).astype(jnp.int32)
        has_new = jnp.sum(is_owner) > 0
        new_start = jnp.sum(is_owner * starts).astype(jnp.int32)
        new_length = jnp.sum(is_owner * prompt_lengths).astype(jnp.int32)
        slice_start = jnp.clip(new_start, 0, prompt_total - MAXLEN).astype(jnp.int32)
        context_keys = lax.dynamic_slice_in_dim(prompt_keys, slice_start, MAXLEN, 0)
        context_values = lax.dynamic_slice_in_dim(prompt_values, slice_start, MAXLEN, 0)
        offset = new_start - slice_start
        lower = jnp.where(has_new, offset, MAXLEN).astype(jnp.int32)
        upper = jnp.where(has_new, offset + new_length, MAXLEN + own_lengths[0]).astype(jnp.int32)
        fresh = attend_slots(step_queries[:1],
                             jnp.concatenate([context_keys, own_keys[0], step_keys[0]], 0)[None],
                             jnp.concatenate([context_values, own_values[0], step_values[0]], 0)[None],
                             lower[None], upper[None], MAXLEN + CACHE_POSITIONS)
        older = attend_slots(step_queries[1:],
                             jnp.concatenate([own_keys[1:], step_keys[1:]], 1),
                             jnp.concatenate([own_values[1:], step_values[1:]], 1),
                             jnp.zeros_like(own_lengths[1:]), own_lengths[1:], CACHE_POSITIONS)
        return jnp.concatenate([fresh, older], 0).reshape(REQ_DEV * STEPS, -1)

    decode = lax.map(decode_owner, (jnp.arange(N_DP, dtype=jnp.int32), decode_queries, decode_keys, decode_values,
                                    owner_cache_keys, owner_cache_values, owner_lengths)).reshape(prompt_total, -1)
    mixed = jnp.concatenate([prefill, decode], 0)
    group_width = QUERY_HEADS * HEAD_SIZE // N_TENSOR

    def add_group(group_index, summed):
        head_cols = lax.dynamic_slice_in_dim(mixed, group_index * group_width, group_width, 1)
        weight_rows = lax.dynamic_slice_in_dim(out_weight, group_index * group_width, group_width, 0)
        partial_sum = jnp.dot(head_cols, weight_rows, preferred_element_type=jnp.float32).astype(jnp.bfloat16)
        partial_sum = lax.optimization_barrier(partial_sum)
        return summed + partial_sum.astype(jnp.float32)

    summed = lax.fori_loop(0, N_TENSOR, add_group, jnp.zeros((2 * prompt_total, D), jnp.float32))
    return summed.astype(jnp.bfloat16)
```

```python
import functools

import jax
import jax.numpy as jnp
from jax import lax
from jax.experimental import pallas as pl
from jax.experimental.pallas import tpu as pltpu
from jax.sharding import PartitionSpec as P

HEAD_SIZE = 128
STEPS = 4
MAXLEN = 2048
GROUP = 8
WIDE = GROUP * HEAD_SIZE
ROWS = 128
KEYS = 512
SLOTS = 8

masked_score = -1e30
SCALE = HEAD_SIZE ** (-0.5)
SCALE2 = SCALE * 1.4426950408889634
VMEM = 48 * 1024 * 1024
NT = (((1,), (1,)), ((), ()))


def stacked_heads(q_ref, rows, heads):
    return jnp.concatenate(
        [q_ref[rows, g * HEAD_SIZE : (g + 1) * HEAD_SIZE] for g in heads], axis=0
    )


def prefill_kernel(bounds_ref, qpos_ref, qstart_ref, q_ref, k_ref, v_ref, o_ref, m_ref, acc_ref, vx_ref, *, row_base):
    step = pl.program_id(1)
    chunk = row_base + step
    window = k_ref.shape[0]
    parts = 2
    per = GROUP // parts

    @pl.when(step == 0)
    def _():
        vx_ref[:, :HEAD_SIZE] = v_ref[...]
        lane = lax.broadcasted_iota(jnp.int32, (window, HEAD_SIZE), 1)
        vx_ref[:, HEAD_SIZE:] = jnp.where(lane == 0, 1.0, 0.0).astype(jnp.bfloat16)

    m_ref[...] = jnp.full_like(m_ref, masked_score)
    acc_ref[...] = jnp.zeros_like(acc_ref)
    low, clear, diagonal, high = [bounds_ref[4 * chunk + i] for i in range(4)]

    def visit(c, masked):
        at = pl.multiple_of(c * KEYS, KEYS)
        keys = k_ref[pl.ds(at, KEYS), :]
        values = vx_ref[pl.ds(at, KEYS), :]
        if masked:
            pos = at + lax.broadcasted_iota(jnp.int32, (ROWS, KEYS), 1)
            allowed = (pos >= qstart_ref[...]) & (pos <= qpos_ref[...])
            bias = jnp.where(allowed, 0.0, masked_score)
            bias = jnp.concatenate([bias] * per, axis=0)
        for part in range(parts):
            q = stacked_heads(q_ref, slice(None), range(part * per, (part + 1) * per))
            s = lax.dot_general(q, keys, NT, preferred_element_type=jnp.float32)
            if masked:
                s = jnp.where(bias < 0, masked_score, s)
            m_old = m_ref[part]
            m_new = jnp.maximum(m_old, jnp.max(s, axis=1, keepdims=True))
            p = jnp.exp2((s - m_new[:, :1]) * SCALE2).astype(jnp.bfloat16)
            alpha = jnp.exp2((m_old - m_new) * SCALE2)
            acc_ref[part] = acc_ref[part] * alpha[:, :1] + lax.dot_general(
                p, values, (((1,), (0,)), ((), ())), preferred_element_type=jnp.float32
            )
            m_ref[part] = m_new

    lax.fori_loop(low, clear, lambda c, _: (visit(c, True), 0)[1], 0)
    lax.fori_loop(clear, diagonal, lambda c, _: (visit(c, False), 0)[1], 0)
    lax.fori_loop(diagonal, high, lambda c, _: (visit(c, True), 0)[1], 0)
    for g in range(GROUP):
        part, rows = g // per, slice((g % per) * ROWS, (g % per + 1) * ROWS)
        total = acc_ref[part, rows, HEAD_SIZE : HEAD_SIZE + 1]
        o_ref[:, g * HEAD_SIZE : (g + 1) * HEAD_SIZE] = (
            acc_ref[part, rows, :HEAD_SIZE] / total
        ).astype(o_ref.dtype)


def prefill_attend(bounds, qpos, qstart, queries, window, first_head, heads, row_base, row_count):
    chunks = row_count // ROWS
    length = window.shape[0]
    parts = 2
    return pl.pallas_call(
        functools.partial(prefill_kernel, row_base=row_base),
        grid_spec=pltpu.PrefetchScalarGridSpec(
            num_scalar_prefetch=1,
            grid=(heads, chunks),
            in_specs=[
                pl.BlockSpec((ROWS, 1), lambda h, i, b: (row_base + i, 0)),
                pl.BlockSpec((ROWS, 1), lambda h, i, b: (row_base + i, 0)),
                pl.BlockSpec((ROWS, WIDE), lambda h, i, b: (row_base + i, first_head + h)),
                pl.BlockSpec((length, HEAD_SIZE), lambda h, i, b: (0, h)),
                pl.BlockSpec((length, HEAD_SIZE), lambda h, i, b: (0, heads + h)),
            ],
            out_specs=pl.BlockSpec((ROWS, WIDE), lambda h, i, b: (i, h)),
            scratch_shapes=[
                pltpu.VMEM((parts, ROWS * GROUP // parts, HEAD_SIZE), jnp.float32),
                pltpu.VMEM((parts, ROWS * GROUP // parts, 2 * HEAD_SIZE), jnp.float32),
                pltpu.VMEM((length, 2 * HEAD_SIZE), jnp.bfloat16),
            ],
        ),
        out_shape=jax.ShapeDtypeStruct((row_count, heads * WIDE), jnp.bfloat16),
        compiler_params=pltpu.CompilerParams(vmem_limit_bytes=VMEM),
        cost_estimate=pl.CostEstimate(
            flops=heads * GROUP * row_count * 2048 * 512,
            bytes_accessed=heads * row_count * WIDE * 4,
            transcendentals=heads * GROUP * row_count * 2048,
        ),
        name="prefill_attend",
    )(bounds, qpos, qstart, queries, window, window)


def decode_kernel(valid_ref, q_ref, k_ref, v_ref, ck_ref, cv_ref, o_ref):
    positions = ck_ref.shape[1]
    rows = SLOTS * STEPS
    held = SLOTS * positions
    stack = rows * GROUP

    def grid_of(shape, axis):
        return lax.broadcasted_iota(jnp.int32, shape, axis)

    row_a = grid_of((stack, held), 0) % rows
    same = row_a // STEPS == grid_of((stack, held), 1) // positions
    row_b = grid_of((stack, rows), 0) % rows
    col_b = grid_of((stack, rows), 1)
    own = (row_b // STEPS == col_b // STEPS) & (col_b <= row_b)
    for part in range(ROWS // rows):
        span = slice(part * rows, (part + 1) * rows)
        slots = slice(part * SLOTS, (part + 1) * SLOTS)
        q = stacked_heads(q_ref, span, range(GROUP))
        cached = ck_ref[slots].reshape(held, HEAD_SIZE)
        cached_values = cv_ref[slots].reshape(held, HEAD_SIZE)
        s_a = lax.dot_general(q, cached, NT, preferred_element_type=jnp.float32)
        s_b = lax.dot_general(q, k_ref[span, :], NT, preferred_element_type=jnp.float32)
        s_a = jnp.where(same & (valid_ref[0, part : part + 1, :] > 0), s_a, masked_score)
        s_b = jnp.where(own, s_b, masked_score)
        top = jnp.maximum(jnp.max(s_a, axis=1, keepdims=True), jnp.max(s_b, axis=1, keepdims=True))
        p_a = jnp.exp2((s_a - top) * SCALE2)
        p_b = jnp.exp2((s_b - top) * SCALE2)
        total = jnp.sum(p_a, axis=1, keepdims=True) + jnp.sum(p_b, axis=1, keepdims=True)
        out = jnp.dot(p_a.astype(jnp.bfloat16), cached_values, preferred_element_type=jnp.float32)
        out += jnp.dot(p_b.astype(jnp.bfloat16), v_ref[span, :], preferred_element_type=jnp.float32)
        out = (out / total).astype(o_ref.dtype)
        for g in range(GROUP):
            o_ref[span, g * HEAD_SIZE : (g + 1) * HEAD_SIZE] = out[g * rows : (g + 1) * rows]


def decode_attend(valid, queries, keys, values, cached_keys, cached_values, first_head, heads, row_base, row_count):
    positions = cached_keys.shape[1]
    slots = ROWS // STEPS
    parts = ROWS // (SLOTS * STEPS)
    return pl.pallas_call(
        decode_kernel,
        grid=(heads, row_count // ROWS),
        in_specs=[
            pl.BlockSpec((1, parts, SLOTS * positions), lambda h, i: (row_base + i, 0, 0)),
            pl.BlockSpec((ROWS, WIDE), lambda h, i: (row_base + i, first_head + h)),
            pl.BlockSpec((ROWS, HEAD_SIZE), lambda h, i: (row_base + i, first_head + h)),
            pl.BlockSpec((ROWS, HEAD_SIZE), lambda h, i: (row_base + i, first_head + h)),
            pl.BlockSpec((slots, positions, HEAD_SIZE), lambda h, i: (row_base + i, 0, first_head + h)),
            pl.BlockSpec((slots, positions, HEAD_SIZE), lambda h, i: (row_base + i, 0, first_head + h)),
        ],
        out_specs=pl.BlockSpec((ROWS, WIDE), lambda h, i: (i, h)),
        out_shape=jax.ShapeDtypeStruct((row_count, heads * WIDE), jnp.bfloat16),
        compiler_params=pltpu.CompilerParams(vmem_limit_bytes=VMEM),
        cost_estimate=pl.CostEstimate(
            flops=heads * GROUP * row_count * 2048 * 512,
            bytes_accessed=heads * row_count * WIDE * 4,
            transcendentals=heads * GROUP * row_count * 2048,
        ),
        name="decode_attend",
    )(valid, queries, keys, values, cached_keys, cached_values)


def project_kernel(base_ref, *refs):
    parts, w_ref, o_ref = refs[:-2], refs[-2], refs[-1]
    total, depth = None, 0
    for part in parts:
        count = part.shape[1]
        product = jnp.dot(
            part[...], w_ref[depth : depth + count, :], preferred_element_type=jnp.float32
        )
        total = product if total is None else total + product
        depth += count
    o_ref[...] = total.astype(o_ref.dtype)


def project(parts, row_blocks, row_count, weight, base, columns):
    tile = [c for c in (512, 640, 256, 128) if columns % c == 0][0]
    tiles = columns // tile
    depth = weight.shape[0]
    specs = [
        pl.BlockSpec((row_count, part.shape[1]), lambda j, b, block=block: (block, 0))
        for part, block in zip(parts, row_blocks)
    ]
    return pl.pallas_call(
        project_kernel,
        grid_spec=pltpu.PrefetchScalarGridSpec(
            num_scalar_prefetch=1,
            grid=(tiles,),
            in_specs=specs + [pl.BlockSpec((depth, tile), lambda j, b: (0, b[0] * tiles + j))],
            out_specs=pl.BlockSpec((row_count, tile), lambda j, b: (0, j)),
        ),
        out_shape=jax.ShapeDtypeStruct((row_count, columns), jnp.bfloat16),
        compiler_params=pltpu.CompilerParams(vmem_limit_bytes=VMEM),
        cost_estimate=pl.CostEstimate(
            flops=2 * row_count * depth * columns,
            bytes_accessed=2 * depth * columns,
            transcendentals=0,
        ),
        name="project",
    )(base, *parts, weight)


def on_device(
    query_rows,
    key_rows,
    rows_of_values,
    cached_key_rows,
    cached_value_rows,
    cache_lengths,
    prompt_lengths,
    owners,
    out_weight,
):
    row_count = query_rows.shape[0]
    count = lax.axis_size("dp")
    heads = key_rows.shape[1] // HEAD_SIZE
    position = lax.axis_index("dp")
    section = lax.axis_index("section")
    first_section = section == 0
    core = position % 2
    chip = position // 2
    first_row = position * row_count
    starts = jnp.cumsum(prompt_lengths) - prompt_lengths
    ends = starts + prompt_lengths

    def up(array, by):
        return lax.ppermute(array, ("section", "dp"), [(i, i + by) for i in range(count - by)])

    def partner(array):
        return lax.ppermute(array, ("section", "dp"), [(i, i ^ 1) for i in range(count)])

    def across(array):
        return lax.ppermute(array, ("section", "dp"), [(i, i + count) for i in range(count)])

    split = [heads // 2, heads - heads // 2] if heads > 1 else [heads]
    packed, first = [], 0
    for width in split:
        cols = slice(first * HEAD_SIZE, (first + width) * HEAD_SIZE)
        packed.append(jnp.concatenate([key_rows[:, cols], rows_of_values[:, cols]], 1))
        first += width

    reach = MAXLEN // row_count
    hops = -(-reach // 2)

    def window_of(block):
        far = [up(block, 2 * hop) for hop in range(hops, 0, -1)] + [block]
        pieces = []
        for piece in far:
            other = partner(piece)
            pieces += [jnp.where(core == 0, piece, other), jnp.where(core == 0, other, piece)]
        return jnp.concatenate(pieces, 0)

    windows = [window_of(block) for block in packed]
    window_start = (chip - hops) * 2 * row_count

    prompt_block = [across(block) for block in packed]
    gathered = lax.all_gather(query_rows[:STEPS], "dp", axis=0, tiled=False)
    row = first_row + jnp.arange(row_count, dtype=jnp.int32)
    inside = (row[None] >= starts[:, None]) & (row[None] < ends[:, None])
    owner_of_row = jnp.sum(jnp.where(inside, owners[:, None], 0), axis=0)

    def fresh_part():
        keys = jnp.concatenate([b[:, : b.shape[1] // 2] for b in prompt_block], 1)
        values = jnp.concatenate([b[:, b.shape[1] // 2 :] for b in prompt_block], 1)
        keys = keys.reshape(row_count, heads, HEAD_SIZE)
        values = values.reshape(row_count, heads, HEAD_SIZE)
        q = gathered.reshape(count, STEPS, heads, GROUP, HEAD_SIZE)
        s = jnp.einsum("oskgd,wkd->kosgw", q, keys, preferred_element_type=jnp.float32) * SCALE
        ok = owner_of_row[None] == jnp.arange(count, dtype=jnp.int32)[:, None]
        ok = ok[None, :, None, None, :]
        s = jnp.where(ok, s, masked_score)
        top = jnp.max(s, axis=-1)
        p = jnp.where(ok, jnp.exp(s - top[..., None]), 0.0)
        total = jnp.sum(p, axis=-1)
        out = jnp.einsum(
            "kosgw,wkd->oskgd", p.astype(jnp.bfloat16), values, preferred_element_type=jnp.float32
        )
        top = jnp.transpose(top, (1, 2, 0, 3)).reshape(count, STEPS, -1)
        total = jnp.transpose(total, (1, 2, 0, 3)).reshape(count, STEPS, -1)
        return jnp.concatenate([out.reshape(count, STEPS, -1), top, total], -1)

    q_heads = heads * GROUP
    packet = q_heads * (HEAD_SIZE + 2)
    partials = lax.cond(
        first_section, lambda: jnp.zeros((count, STEPS, packet), jnp.float32), fresh_part
    )
    mine = [lax.dynamic_index_in_dim(partials, position, 0, keepdims=False)]
    for by in range(1, count):
        sent = lax.dynamic_index_in_dim(partials, (position + by) % count, 0, keepdims=False)
        mine.append(
            lax.ppermute(
                sent,
                ("section", "dp"),
                [(count + i, count + (i + by) % count) for i in range(count)],
            )
        )

    def fresh_rows():
        parts = jnp.stack(mine)
        outs = parts[..., : q_heads * HEAD_SIZE].reshape(count, STEPS, q_heads, HEAD_SIZE)
        tops = parts[..., q_heads * HEAD_SIZE : q_heads * (HEAD_SIZE + 1)]
        totals = parts[..., q_heads * (HEAD_SIZE + 1) :]
        has_new = jnp.sum((owners == position).astype(jnp.int32)) > 0
        cache_size = cached_key_rows.shape[1]
        keys = jnp.concatenate([cached_key_rows[0], key_rows[:STEPS]], 0).reshape(-1, heads, HEAD_SIZE)
        values = jnp.concatenate([cached_value_rows[0], rows_of_values[:STEPS]], 0)
        values = values.reshape(-1, heads, HEAD_SIZE)
        q = query_rows[:STEPS].reshape(STEPS, heads, GROUP, HEAD_SIZE)
        s = jnp.einsum("skgd,wkd->skgw", q, keys, preferred_element_type=jnp.float32) * SCALE
        pos = jnp.arange(cache_size + STEPS, dtype=jnp.int32)
        limit = jnp.where(has_new, 0, cache_lengths[0])
        ok = (pos[None] < jnp.minimum(limit, cache_size)) | (
            (pos[None] >= cache_size)
            & (pos[None] - cache_size <= jnp.arange(STEPS, dtype=jnp.int32)[:, None])
        )
        s = jnp.where(ok[:, None, None, :], s, masked_score).reshape(STEPS, q_heads, -1)
        top = jnp.maximum(jnp.max(s, axis=-1), jnp.max(tops, axis=0))
        p = jnp.exp(s - top[..., None])
        gains = jnp.where(totals > 0, jnp.exp(jnp.minimum(tops - top, 0.0)), 0.0)
        total = jnp.sum(p, axis=-1) + jnp.sum(totals * gains, axis=0)
        out = jnp.einsum(
            "skgw,wkd->skgd",
            p.astype(jnp.bfloat16).reshape(STEPS, heads, GROUP, -1),
            values,
            preferred_element_type=jnp.float32,
        ).reshape(STEPS, q_heads, HEAD_SIZE)
        out = out + jnp.sum(outs * gains[..., None], axis=0)
        return (out / total[..., None]).astype(jnp.bfloat16).reshape(STEPS, -1)

    query_start = jnp.max(jnp.where(starts[None, :] <= row[:, None], starts[None, :], 0), axis=1)
    qpos = (row - window_start)[:, None]
    qstart = (query_start - window_start)[:, None]
    by_chunk = (query_start - window_start).reshape(-1, ROWS)
    chunk_first = row.reshape(-1, ROWS)[:, 0] - window_start
    high = (chunk_first + ROWS - 1) // KEYS + 1
    low = jnp.clip(jnp.min(by_chunk, axis=1) // KEYS, 0, high)
    clear = jnp.clip((jnp.max(by_chunk, axis=1) + KEYS - 1) // KEYS, low, high)
    diagonal = jnp.clip(chunk_first // KEYS, clear, high)
    bounds = jnp.stack([low, clear, diagonal, high], 1).reshape(-1).astype(jnp.int32)

    cache_size = cached_key_rows.shape[1]
    valid = jnp.arange(cache_size, dtype=jnp.int32)[None] < cache_lengths[:, None]
    valid = valid.astype(jnp.float32).reshape(row_count // ROWS, -1, SLOTS * cache_size)

    def attend(half, row_base, rows, tied=None):
        first_head = sum(split[:half])
        width = split[half]

        def prefill():
            return prefill_attend(
                bounds, qpos, qstart, query_rows, windows[half], first_head, width, row_base, rows
            )

        def decode():
            out = decode_attend(
                valid, query_rows, key_rows, rows_of_values, cached_key_rows, cached_value_rows,
                first_head, width, row_base, rows,
            )
            return out

        return lax.cond(first_section, prefill, decode)

    def with_fresh(out, half):
        first_head = sum(split[:half])
        cols = slice(first_head * WIDE, (first_head + split[half]) * WIDE)
        rows = jnp.where(first_section, out[:STEPS], fresh[:, cols])
        return lax.dynamic_update_slice(out, rows, (0, 0))

    early = [attend(0, 0, row_count)] if len(split) > 1 else []
    fresh = lax.cond(
        first_section, lambda: jnp.zeros((STEPS, q_heads * HEAD_SIZE), jnp.bfloat16), fresh_rows
    )
    early = [with_fresh(early[0], 0)] if early else []
    ranks = lax.axis_size("tensor")
    rank = lax.axis_index("tensor")
    columns = out_weight.shape[1] // ranks
    half_rows = row_count // 2
    done = []
    for block in range(2):
        late = attend(len(split) - 1, block * half_rows // ROWS, half_rows)
        if block == 0:
            late = with_fresh(late, len(split) - 1)
        parts = early + [late]
        blocks = [block] * len(early) + [0]
        arrived = []
        for by in range(1, ranks):
            to = (rank + by) % ranks
            part = project(parts, blocks, half_rows, out_weight, to.reshape(1), columns)
            arrived.append(
                lax.ppermute(part, "tensor", [(i, (i + by) % ranks) for i in range(ranks)])
            )
        own = project(parts, blocks, half_rows, out_weight, rank.reshape(1), columns)
        done.append((own, arrived))
    outs = []
    for own, arrived in done:
        total = own.astype(jnp.float32)
        for part in arrived:
            total = total + part.astype(jnp.float32)
        outs.append(total.astype(jnp.bfloat16))
    return jnp.concatenate(outs, 0)


def solution(mesh):
    placed = (
        P(("section", "dp"), "tensor"),
        P(("section", "dp"), "tensor"),
        P(("section", "dp"), "tensor"),
        P("dp", None, "tensor"),
        P("dp", None, "tensor"),
        P("dp"),
        P(),
        P(),
        P("tensor", None),
    )
    return jax.shard_map(
        on_device,
        mesh=mesh,
        in_specs=placed,
        out_specs=P(("section", "dp"), "tensor"),
        check_vma=False,
    )
```

```python
import functools

import jax
import jax.numpy as jnp
from jax import lax
from jax.experimental import pallas as pl
from jax.experimental.pallas import tpu as pltpu
from jax.sharding import PartitionSpec as P

HEAD_SIZE = 128
STEPS = 4
MAXLEN = 2048
GROUP = 8
WIDE = GROUP * HEAD_SIZE
ROWS = 256
KEYS = 512
PARTS = 8
SLOTS = 8

masked_score = -1e30
SCALE = HEAD_SIZE ** (-0.5)
SCALE2 = SCALE * 1.4426950408889634
VMEM = 48 * 1024 * 1024
NT = (((1,), (1,)), ((), ()))


def stacked_heads(q_ref, rows, heads):
    return jnp.concatenate(
        [q_ref[rows, g * HEAD_SIZE : (g + 1) * HEAD_SIZE] for g in heads], axis=0
    )


def prefill_kernel(bounds_ref, qpos_ref, qstart_ref, q_ref, k_ref, v_ref, o_ref, m_ref, acc_ref, vx_ref, *, row_base):
    step = pl.program_id(1)
    chunk = row_base + step
    window = k_ref.shape[0]
    parts = PARTS
    per = GROUP // parts

    @pl.when(step == 0)
    def _():
        vx_ref[:, :HEAD_SIZE] = v_ref[...]
        lane = lax.broadcasted_iota(jnp.int32, (window, HEAD_SIZE), 1)
        vx_ref[:, HEAD_SIZE:] = jnp.where(lane == 0, 1.0, 0.0).astype(jnp.bfloat16)

    m_ref[...] = jnp.full_like(m_ref, masked_score)
    acc_ref[...] = jnp.zeros_like(acc_ref)
    low, clear, diagonal, high = [bounds_ref[4 * chunk + i] for i in range(4)]

    def visit(c, masked):
        at = pl.multiple_of(c * KEYS, KEYS)
        keys = k_ref[pl.ds(at, KEYS), :]
        values = vx_ref[pl.ds(at, KEYS), :]
        if masked:
            pos = at + lax.broadcasted_iota(jnp.int32, (ROWS, KEYS), 1)
            allowed = (pos >= qstart_ref[...]) & (pos <= qpos_ref[...])
            bias = jnp.where(allowed, 0.0, masked_score)
            bias = jnp.concatenate([bias] * per, axis=0)
        for part in range(parts):
            q = stacked_heads(q_ref, slice(None), range(part * per, (part + 1) * per))
            s = lax.dot_general(q, keys, NT, preferred_element_type=jnp.float32)
            if masked:
                s = jnp.where(bias < 0, masked_score, s)
            m_old = m_ref[part]
            m_new = jnp.maximum(m_old, jnp.max(s, axis=1, keepdims=True))
            p = jnp.exp2((s - jnp.concatenate([m_new] * (KEYS // HEAD_SIZE), 1)) * SCALE2)
            p = p.astype(jnp.bfloat16)
            alpha = jnp.exp2((m_old - m_new) * SCALE2)
            acc_ref[part] = acc_ref[part] * jnp.concatenate([alpha] * 2, 1) + lax.dot_general(
                p, values, (((1,), (0,)), ((), ())), preferred_element_type=jnp.float32
            )
            m_ref[part] = m_new

    lax.fori_loop(low, clear, lambda c, _: (visit(c, True), 0)[1], 0)
    lax.fori_loop(clear, diagonal, lambda c, _: (visit(c, False), 0)[1], 0)
    lax.fori_loop(diagonal, high, lambda c, _: (visit(c, True), 0)[1], 0)
    for g in range(GROUP):
        part, rows = g // per, slice((g % per) * ROWS, (g % per + 1) * ROWS)
        total = acc_ref[part, rows, HEAD_SIZE : HEAD_SIZE + 1]
        o_ref[:, g * HEAD_SIZE : (g + 1) * HEAD_SIZE] = (
            acc_ref[part, rows, :HEAD_SIZE] / total
        ).astype(o_ref.dtype)


def prefill_attend(bounds, qpos, qstart, queries, window, first_head, heads, row_base, row_count):
    chunks = row_count // ROWS
    length = window.shape[0]
    parts = PARTS
    return pl.pallas_call(
        functools.partial(prefill_kernel, row_base=row_base),
        grid_spec=pltpu.PrefetchScalarGridSpec(
            num_scalar_prefetch=1,
            grid=(heads, chunks),
            in_specs=[
                pl.BlockSpec((ROWS, 1), lambda h, i, b: (row_base + i, 0)),
                pl.BlockSpec((ROWS, 1), lambda h, i, b: (row_base + i, 0)),
                pl.BlockSpec((ROWS, WIDE), lambda h, i, b: (row_base + i, first_head + h)),
                pl.BlockSpec((length, HEAD_SIZE), lambda h, i, b: (0, h)),
                pl.BlockSpec((length, HEAD_SIZE), lambda h, i, b: (0, heads + h)),
            ],
            out_specs=pl.BlockSpec((ROWS, WIDE), lambda h, i, b: (i, h)),
            scratch_shapes=[
                pltpu.VMEM((parts, ROWS * GROUP // parts, HEAD_SIZE), jnp.float32),
                pltpu.VMEM((parts, ROWS * GROUP // parts, 2 * HEAD_SIZE), jnp.float32),
                pltpu.VMEM((length, 2 * HEAD_SIZE), jnp.bfloat16),
            ],
        ),
        out_shape=jax.ShapeDtypeStruct((row_count, heads * WIDE), jnp.bfloat16),
        compiler_params=pltpu.CompilerParams(vmem_limit_bytes=VMEM),
        cost_estimate=pl.CostEstimate(
            flops=heads * GROUP * row_count * 2048 * 512,
            bytes_accessed=heads * row_count * WIDE * 4,
            transcendentals=heads * GROUP * row_count * 2048,
        ),
        name="prefill_attend",
    )(bounds, qpos, qstart, queries, window, window)


def decode_kernel(valid_ref, q_ref, k_ref, v_ref, ck_ref, cv_ref, o_ref):
    positions = ck_ref.shape[1]
    rows = SLOTS * STEPS
    held = SLOTS * positions
    stack = rows * GROUP

    def grid_of(shape, axis):
        return lax.broadcasted_iota(jnp.int32, shape, axis)

    row_a = grid_of((stack, held), 0) % rows
    same = row_a // STEPS == grid_of((stack, held), 1) // positions
    row_b = grid_of((stack, rows), 0) % rows
    col_b = grid_of((stack, rows), 1)
    own = (row_b // STEPS == col_b // STEPS) & (col_b <= row_b)
    for part in range(ROWS // rows):
        span = slice(part * rows, (part + 1) * rows)
        slots = slice(part * SLOTS, (part + 1) * SLOTS)
        q = stacked_heads(q_ref, span, range(GROUP))
        cached = ck_ref[slots].reshape(held, HEAD_SIZE)
        cached_values = cv_ref[slots].reshape(held, HEAD_SIZE)
        s_a = lax.dot_general(q, cached, NT, preferred_element_type=jnp.float32)
        s_b = lax.dot_general(q, k_ref[span, :], NT, preferred_element_type=jnp.float32)
        s_a = jnp.where(same & (valid_ref[0, part : part + 1, :] > 0), s_a, masked_score)
        s_b = jnp.where(own, s_b, masked_score)
        top = jnp.maximum(jnp.max(s_a, axis=1, keepdims=True), jnp.max(s_b, axis=1, keepdims=True))
        p_a = jnp.exp2((s_a - top) * SCALE2)
        p_b = jnp.exp2((s_b - top) * SCALE2)
        total = jnp.sum(p_a, axis=1, keepdims=True) + jnp.sum(p_b, axis=1, keepdims=True)
        out = jnp.dot(p_a.astype(jnp.bfloat16), cached_values, preferred_element_type=jnp.float32)
        out += jnp.dot(p_b.astype(jnp.bfloat16), v_ref[span, :], preferred_element_type=jnp.float32)
        out = (out / total).astype(o_ref.dtype)
        for g in range(GROUP):
            o_ref[span, g * HEAD_SIZE : (g + 1) * HEAD_SIZE] = out[g * rows : (g + 1) * rows]


def decode_attend(valid, queries, keys, values, cached_keys, cached_values, first_head, heads, row_base, row_count):
    positions = cached_keys.shape[1]
    slots = ROWS // STEPS
    parts = ROWS // (SLOTS * STEPS)
    return pl.pallas_call(
        decode_kernel,
        grid=(heads, row_count // ROWS),
        in_specs=[
            pl.BlockSpec((1, parts, SLOTS * positions), lambda h, i: (row_base + i, 0, 0)),
            pl.BlockSpec((ROWS, WIDE), lambda h, i: (row_base + i, first_head + h)),
            pl.BlockSpec((ROWS, HEAD_SIZE), lambda h, i: (row_base + i, first_head + h)),
            pl.BlockSpec((ROWS, HEAD_SIZE), lambda h, i: (row_base + i, first_head + h)),
            pl.BlockSpec((slots, positions, HEAD_SIZE), lambda h, i: (row_base + i, 0, first_head + h)),
            pl.BlockSpec((slots, positions, HEAD_SIZE), lambda h, i: (row_base + i, 0, first_head + h)),
        ],
        out_specs=pl.BlockSpec((ROWS, WIDE), lambda h, i: (i, h)),
        out_shape=jax.ShapeDtypeStruct((row_count, heads * WIDE), jnp.bfloat16),
        compiler_params=pltpu.CompilerParams(vmem_limit_bytes=VMEM),
        cost_estimate=pl.CostEstimate(
            flops=heads * GROUP * row_count * 2048 * 512,
            bytes_accessed=heads * row_count * WIDE * 4,
            transcendentals=heads * GROUP * row_count * 2048,
        ),
        name="decode_attend",
    )(valid, queries, keys, values, cached_keys, cached_values)


def project_kernel(base_ref, *refs):
    parts, w_ref, o_ref = refs[:-2], refs[-2], refs[-1]
    total, depth = None, 0
    for part in parts:
        count = part.shape[1]
        product = jnp.dot(
            part[...], w_ref[depth : depth + count, :], preferred_element_type=jnp.float32
        )
        total = product if total is None else total + product
        depth += count
    o_ref[...] = total.astype(o_ref.dtype)


def project(parts, row_blocks, row_count, weight, base, columns):
    tile = [c for c in (512, 640, 256, 128) if columns % c == 0][0]
    tiles = columns // tile
    depth = weight.shape[0]
    specs = [
        pl.BlockSpec((row_count, part.shape[1]), lambda j, b, block=block: (block, 0))
        for part, block in zip(parts, row_blocks)
    ]
    return pl.pallas_call(
        project_kernel,
        grid_spec=pltpu.PrefetchScalarGridSpec(
            num_scalar_prefetch=1,
            grid=(tiles,),
            in_specs=specs + [pl.BlockSpec((depth, tile), lambda j, b: (0, b[0] * tiles + j))],
            out_specs=pl.BlockSpec((row_count, tile), lambda j, b: (0, j)),
        ),
        out_shape=jax.ShapeDtypeStruct((row_count, columns), jnp.bfloat16),
        compiler_params=pltpu.CompilerParams(vmem_limit_bytes=VMEM),
        cost_estimate=pl.CostEstimate(
            flops=2 * row_count * depth * columns,
            bytes_accessed=2 * depth * columns,
            transcendentals=0,
        ),
        name="project",
    )(base, *parts, weight)


def on_device(
    query_rows,
    key_rows,
    rows_of_values,
    cached_key_rows,
    cached_value_rows,
    cache_lengths,
    prompt_lengths,
    owners,
    out_weight,
):
    row_count = query_rows.shape[0]
    count = lax.axis_size("dp")
    heads = key_rows.shape[1] // HEAD_SIZE
    position = lax.axis_index("dp")
    section = lax.axis_index("section")
    first_section = section == 0
    core = position % 2
    chip = position // 2
    first_row = position * row_count
    starts = jnp.cumsum(prompt_lengths) - prompt_lengths
    ends = starts + prompt_lengths

    def up(array, by):
        return lax.ppermute(array, ("section", "dp"), [(i, i + by) for i in range(count - by)])

    def partner(array):
        return lax.ppermute(array, ("section", "dp"), [(i, i ^ 1) for i in range(count)])

    def across(array):
        return lax.ppermute(array, ("section", "dp"), [(i, i + count) for i in range(count)])

    split = [heads // 2, heads - heads // 2] if heads > 1 else [heads]
    packed, first = [], 0
    for width in split:
        cols = slice(first * HEAD_SIZE, (first + width) * HEAD_SIZE)
        packed.append(jnp.concatenate([key_rows[:, cols], rows_of_values[:, cols]], 1))
        first += width

    reach = MAXLEN // row_count
    hops = -(-reach // 2)

    def lifted(block):
        return [up(block, 2 * hop) for hop in range(hops, 0, -1)]

    def window_of(far, block):
        pieces = []
        for piece in far + [block]:
            other = partner(piece)
            pieces += [jnp.where(core == 0, piece, other), jnp.where(core == 0, other, piece)]
        return jnp.concatenate(pieces, 0)

    window_start = (chip - hops) * 2 * row_count

    prompt_block = [across(block) for block in packed]
    first_queries = query_rows[:STEPS]
    around = [first_queries] + [
        lax.ppermute(
            first_queries,
            ("section", "dp"),
            [(count + i, count + (i - by) % count) for i in range(count)],
        )
        for by in range(1, count)
    ]
    row = first_row + jnp.arange(row_count, dtype=jnp.int32)
    inside = (row[None] >= starts[:, None]) & (row[None] < ends[:, None])
    owner_of_row = jnp.sum(jnp.where(inside, owners[:, None], 0), axis=0)

    def fresh_part():
        keys = jnp.concatenate([b[:, : b.shape[1] // 2] for b in prompt_block], 1)
        values = jnp.concatenate([b[:, b.shape[1] // 2 :] for b in prompt_block], 1)
        keys = keys.reshape(row_count, heads, HEAD_SIZE)
        values = values.reshape(row_count, heads, HEAD_SIZE)
        q = jnp.stack(around).reshape(count, STEPS, heads, GROUP, HEAD_SIZE)
        s = jnp.einsum("oskgd,wkd->kosgw", q, keys, preferred_element_type=jnp.float32) * SCALE
        asker = (position + jnp.arange(count, dtype=jnp.int32)) % count
        ok = owner_of_row[None] == asker[:, None]
        ok = ok[None, :, None, None, :]
        s = jnp.where(ok, s, masked_score)
        top = jnp.max(s, axis=-1)
        p = jnp.where(ok, jnp.exp(s - top[..., None]), 0.0)
        total = jnp.sum(p, axis=-1)
        out = jnp.einsum(
            "kosgw,wkd->oskgd", p.astype(jnp.bfloat16), values, preferred_element_type=jnp.float32
        )
        top = jnp.transpose(top, (1, 2, 0, 3)).reshape(count, STEPS, -1)
        total = jnp.transpose(total, (1, 2, 0, 3)).reshape(count, STEPS, -1)
        return jnp.concatenate([out.reshape(count, STEPS, -1), top, total], -1)

    q_heads = heads * GROUP
    packet = q_heads * (HEAD_SIZE + 2)
    partials = lax.cond(
        first_section, lambda: jnp.zeros((count, STEPS, packet), jnp.float32), fresh_part
    )
    mine = [partials[0]]
    for by in range(1, count):
        mine.append(
            lax.ppermute(
                partials[by],
                ("section", "dp"),
                [(count + i, count + (i + by) % count) for i in range(count)],
            )
        )

    def fresh_rows():
        parts = jnp.stack(mine)
        outs = parts[..., : q_heads * HEAD_SIZE].reshape(count, STEPS, q_heads, HEAD_SIZE)
        tops = parts[..., q_heads * HEAD_SIZE : q_heads * (HEAD_SIZE + 1)]
        totals = parts[..., q_heads * (HEAD_SIZE + 1) :]
        has_new = jnp.sum((owners == position).astype(jnp.int32)) > 0
        cache_size = cached_key_rows.shape[1]
        keys = jnp.concatenate([cached_key_rows[0], key_rows[:STEPS]], 0).reshape(-1, heads, HEAD_SIZE)
        values = jnp.concatenate([cached_value_rows[0], rows_of_values[:STEPS]], 0)
        values = values.reshape(-1, heads, HEAD_SIZE)
        q = query_rows[:STEPS].reshape(STEPS, heads, GROUP, HEAD_SIZE)
        s = jnp.einsum("skgd,wkd->skgw", q, keys, preferred_element_type=jnp.float32) * SCALE
        pos = jnp.arange(cache_size + STEPS, dtype=jnp.int32)
        limit = jnp.where(has_new, 0, cache_lengths[0])
        ok = (pos[None] < jnp.minimum(limit, cache_size)) | (
            (pos[None] >= cache_size)
            & (pos[None] - cache_size <= jnp.arange(STEPS, dtype=jnp.int32)[:, None])
        )
        s = jnp.where(ok[:, None, None, :], s, masked_score).reshape(STEPS, q_heads, -1)
        top = jnp.maximum(jnp.max(s, axis=-1), jnp.max(tops, axis=0))
        p = jnp.exp(s - top[..., None])
        gains = jnp.where(totals > 0, jnp.exp(jnp.minimum(tops - top, 0.0)), 0.0)
        total = jnp.sum(p, axis=-1) + jnp.sum(totals * gains, axis=0)
        out = jnp.einsum(
            "skgw,wkd->skgd",
            p.astype(jnp.bfloat16).reshape(STEPS, heads, GROUP, -1),
            values,
            preferred_element_type=jnp.float32,
        ).reshape(STEPS, q_heads, HEAD_SIZE)
        out = out + jnp.sum(outs * gains[..., None], axis=0)
        return (out / total[..., None]).astype(jnp.bfloat16).reshape(STEPS, -1)

    query_start = jnp.max(jnp.where(starts[None, :] <= row[:, None], starts[None, :], 0), axis=1)
    qpos = (row - window_start)[:, None]
    qstart = (query_start - window_start)[:, None]
    by_chunk = (query_start - window_start).reshape(-1, ROWS)
    chunk_first = row.reshape(-1, ROWS)[:, 0] - window_start
    high = (chunk_first + ROWS - 1) // KEYS + 1
    low = jnp.clip(jnp.min(by_chunk, axis=1) // KEYS, 0, high)
    clear = jnp.clip((jnp.max(by_chunk, axis=1) + KEYS - 1) // KEYS, low, high)
    diagonal = jnp.clip(chunk_first // KEYS, clear, high)
    bounds = jnp.stack([low, clear, diagonal, high], 1).reshape(-1).astype(jnp.int32)

    cache_size = cached_key_rows.shape[1]
    valid = jnp.arange(cache_size, dtype=jnp.int32)[None] < cache_lengths[:, None]
    valid = valid.astype(jnp.float32).reshape(row_count // ROWS, -1, SLOTS * cache_size)

    def attend(half, window, row_base, rows):
        first_head = sum(split[:half])
        width = split[half]

        def prefill():
            return prefill_attend(
                bounds, qpos, qstart, query_rows, window, first_head, width, row_base, rows
            )

        def decode():
            out = decode_attend(
                valid, query_rows, key_rows, rows_of_values, cached_key_rows, cached_value_rows,
                first_head, width, row_base, rows,
            )
            return out

        return lax.cond(first_section, prefill, decode)

    def with_fresh(out, half):
        first_head = sum(split[:half])
        cols = slice(first_head * WIDE, (first_head + split[half]) * WIDE)
        rows = jnp.where(first_section, out[:STEPS], fresh[:, cols])
        return lax.dynamic_update_slice(out, rows, (0, 0))

    last = len(split) - 1
    if last:
        window = window_of(lifted(packed[0]), packed[0])
        window, block = lax.optimization_barrier((window, packed[1]))
        far = lifted(block)
        early = attend(0, window, 0, row_count)
        early, block = lax.optimization_barrier((early, block))
        window = window_of(lax.optimization_barrier((far, early))[0], block)
    else:
        window = window_of(lifted(packed[0]), packed[0])
    fresh = lax.cond(
        first_section, lambda: jnp.zeros((STEPS, q_heads * HEAD_SIZE), jnp.bfloat16), fresh_rows
    )
    early = [with_fresh(early, 0)] if last else []
    ranks = lax.axis_size("tensor")
    rank = lax.axis_index("tensor")
    columns = out_weight.shape[1] // ranks
    half_rows = row_count // 2
    peers = []
    for block in range(2):
        late = attend(last, window, block * half_rows // ROWS, half_rows)
        if block == 0:
            late = with_fresh(late, last)
        if block == 1:
            landed, late = lax.optimization_barrier((peers[0][2], late))
            peers[0] = peers[0][:2] + (landed,) + peers[0][3:]
        parts = early + [late]
        blocks = [block] * len(early) + [0]
        arrived = []
        for by in range(1, ranks):
            to = (rank + by) % ranks
            part = project(parts, blocks, half_rows, out_weight, to.reshape(1), columns)
            if block == 0:
                part, window = lax.optimization_barrier((part, window))
            arrived.append(
                lax.ppermute(part, "tensor", [(i, (i + by) % ranks) for i in range(ranks)])
            )
        peers.append((parts, blocks, arrived, part if ranks > 1 else None))
    done = []
    for block, (parts, blocks, arrived, _) in enumerate(peers):
        own_rank = rank.reshape(1)
        if ranks > 1:
            own_rank, _ = lax.optimization_barrier((own_rank, peers[1][3]))
        own = project(parts, blocks, half_rows, out_weight, own_rank, columns)
        done.append((own, arrived))
    outs = []
    for own, arrived in done:
        total = own.astype(jnp.float32)
        for part in arrived:
            total = total + part.astype(jnp.float32)
        outs.append(total.astype(jnp.bfloat16))
    return jnp.concatenate(outs, 0)


def solution(mesh):
    placed = (
        P(("section", "dp"), "tensor"),
        P(("section", "dp"), "tensor"),
        P(("section", "dp"), "tensor"),
        P("dp", None, "tensor"),
        P("dp", None, "tensor"),
        P("dp"),
        P(),
        P(),
        P("tensor", None),
    )
    return jax.shard_map(
        on_device,
        mesh=mesh,
        in_specs=placed,
        out_specs=P(("section", "dp"), "tensor"),
        check_vma=False,
    )
```
